256 devices in a mesh: seq: 64 (over z, y, x_hi), fsdp: 4 (over x_lo, core).
Axes of the slice: x: 4 (x_hi: 2, x_lo: 2; x = x_hi * 2 + x_lo), y: 4, z: 8, core: 2. Of those that a mesh axis runs over, the one named last changes fastest.
Arguments:
- queries: bfloat16 [16384, 4096], P('seq', 'fsdp'), may hold values from -6 to 6
- keys: bfloat16 [16384, 4096], P('seq', 'fsdp'), may hold values from -6 to 6
- values: bfloat16 [16384, 4096], P('seq', 'fsdp'), may hold values from -6 to 6
- filters: float32 [16384, 4096], P('seq', 'fsdp'), as said below
- skip_weight: float32 [4096], P('fsdp'), may hold values from -4 to 4
- out_weight: bfloat16 [4096, 4096], P('fsdp'), may hold values from -0.125 to 0.125
Outputs:
- mixed_out: bfloat16 [16384, 4096], P('seq', 'fsdp')
The draws below stay inside these ranges and needn't reach their ends.
Inputs may be any that keep to these rules, and one draw needn't show every extreme that they name: `filters`: real filter values of the 4096 channels at 16384 lags.
All inputs are finite; a program needn't handle non-finite values.
Results may differ from the reference program's by a relative error of at most 0.0049.
Values may be sent and summed in bfloat16 or wider, within the bound.
A program may use at most 128 MiB of HBM per device.

```python
import math
import jax
import jax.numpy as jnp
from jax import lax

D = 4096
SEQ_LEN = 16384


def draw_filters(key, part):
    sampler_starting_states = jax.random.split(key, 6)
    kernel_span_size = SEQ_LEN
    shift_reach_coordinate = jnp.arange(kernel_span_size, dtype=jnp.float32)[:, None]
    slow_share = 0.5
    is_slow = jax.random.uniform(sampler_starting_states[0], (D,)) < slow_share
    slow_rate = jnp.exp(jax.random.uniform(sampler_starting_states[1], (D,), minval=math.log(0.3 / kernel_span_size), maxval=math.log(2.3 / kernel_span_size)))
    fast_rate = jnp.exp(jax.random.uniform(sampler_starting_states[2], (D,), minval=math.log(1.0 / 50.0), maxval=math.log(1.0 / 30.0)))
    damping_speed = jnp.where(is_slow, slow_rate, fast_rate)[None, :]
    gaussian_jitter = jnp.clip(jax.random.normal(sampler_starting_states[3], (kernel_span_size, D)), -6.0, 6.0)
    impulse_displacements = jax.random.randint(sampler_starting_states[4], (3,), 1, kernel_span_size).astype(jnp.float32)
    impulse_keepers = jax.random.uniform(sampler_starting_states[5], (3,), minval=0.5, maxval=0.8)
    impulse_happenings = jnp.ones((kernel_span_size, 1), jnp.float32)
    for element_number in range(3):
        impulse_happenings = impulse_happenings * jnp.where(shift_reach_coordinate >= impulse_displacements[element_number], impulse_keepers[element_number], 1.0)
    envelope_kernel = gaussian_jitter * jnp.sqrt(2.0 * damping_speed) * jnp.exp(-damping_speed * shift_reach_coordinate) * impulse_happenings
    return envelope_kernel.astype(jnp.float32)


def spiked(drawn, rng, source, target, parts, factor):
    owner, partner = [(jnp.arange(drawn.shape[position]) // (drawn.shape[position] // parts)).reshape([-1 if axis == position else 1 for axis in range(drawn.ndim)]) for position in (source, target)]
    chosen = jax.random.permutation(rng, parts)[partner]
    strong = (owner == chosen) | (owner == (partner + parts // 2) % parts)
    return jnp.where(strong, factor * drawn, drawn)


def level_of(key, shape, cuts, least, largest):
    def one(axis_at, blocks):
        heights = jax.random.uniform(jax.random.fold_in(jax.random.fold_in(key, 6), axis_at), (blocks,), jnp.float32, least / len(cuts), largest / len(cuts))
        return jnp.repeat(jnp.exp(heights), shape[axis_at] // blocks).reshape((-1,) + (1,) * (len(shape) - axis_at - 1))

    level = one(*cuts[0])
    for cut in cuts[1:]:
        level = level * one(*cut)
    return level


def noise(rng, dims, deviation, bound, cuts=(), held_as=jnp.bfloat16):
    entries = jax.random.normal(rng, dims, jnp.float32) * deviation
    if len(cuts) > 0:
        entries = level_of(rng, dims, cuts, -0.22, 0.18) * entries
    return jnp.clip(entries, min=-bound, max=bound).astype(held_as)


def noise_with(rng, dims, scale, bound, pieces, heavy, kind=jnp.bfloat16):
    drawn = scale * jax.random.normal(rng, dims, jnp.float32)
    if pieces:
        drawn = drawn * level_of(rng, dims, pieces, -0.22, 0.18)
    return jnp.clip(spiked(drawn, jax.random.fold_in(rng, 3), *heavy), -bound, bound).astype(kind)


def setup_inputs(seed: int = 0) -> dict:
    streams_of = jax.random.split(jax.random.key(seed), 7)
    return {
        "queries": noise(streams_of[0], (SEQ_LEN, D), 1.0, 6.0, ((0, 64), (1, 4))),
        "keys": noise(streams_of[1], (SEQ_LEN, D), 1.0, 6.0, ((0, 64), (1, 4))),
        "values": noise(streams_of[2], (SEQ_LEN, D), 1.0, 6.0, ((0, 64), (1, 4))),
        "filters": draw_filters(jax.random.fold_in(streams_of[6], 71), 0),
        "skip_weight": noise(streams_of[4], (D,), 1.0, 4.0, ((0, 4),), jnp.float32),
        "out_weight": noise_with(streams_of[5], (D, D), D ** -0.5, 0.125, ((0, 4),), (0, 1, 4, 2.0)),
    }


def convolve_block(block):
    signal, kernel = block
    kernel_span_size = signal.shape[0]
    spectrum = jnp.fft.rfft(signal, 2 * kernel_span_size, axis=0) * jnp.fft.rfft(kernel, 2 * kernel_span_size, axis=0)
    return jnp.fft.irfft(spectrum, 2 * kernel_span_size, axis=0)[:kernel_span_size].astype(signal.dtype)


def reference(queries, keys, values, filters, skip_weight, out_weight):
    product = keys.astype(jnp.float32) * values.astype(jnp.float32)
    width = product.shape[1]
    block_width = min(width, 256)
    block_tally = width // block_width
    kernel_span_size = product.shape[0]
    signal = product.reshape(kernel_span_size, block_tally, block_width).transpose(1, 0, 2)
    kernel = filters.reshape(kernel_span_size, block_tally, block_width).transpose(1, 0, 2)
    conv = lax.map(convolve_block, (signal, kernel))
    conv = conv.transpose(1, 0, 2).reshape(kernel_span_size, width)
    mixed = conv + skip_weight[None, :] * product
    gated = (queries.astype(jnp.float32) * mixed).astype(jnp.bfloat16)
    return jnp.dot(gated, out_weight, preferred_element_type=jnp.float32).astype(jnp.bfloat16)
```

```python
import functools
import math

import jax
import jax.numpy as jnp
import ml_dtypes
import numpy as np
from jax import lax
from jax.experimental import pallas as pl
from jax.experimental.pallas import tpu as pltpu
from jax.sharding import PartitionSpec as P

MESH = pl.DeviceIdType.MESH
BF = jnp.bfloat16
F32 = jnp.float32
GROUP = 4


def split_np(table):
    high = table.astype(np.float32).astype(ml_dtypes.bfloat16)
    low = (table - high.astype(np.float64)).astype(np.float32).astype(ml_dtypes.bfloat16)
    return high, low


def make_tables(n_blocks, width):
    half = width // 2
    total = n_blocks * width
    theta = np.arange(n_blocks) + 0.25
    blocks = np.arange(n_blocks)
    lanes = np.arange(width)
    outer = 2 * math.pi * np.outer(theta, blocks) / n_blocks
    twist = 2 * math.pi * np.outer(theta, lanes) / total
    inner = 2 * math.pi * (np.outer(lanes, lanes) % width) / width
    cos, sin = np.cos(inner), np.sin(inner)
    fwd = np.block([[cos, -sin], [sin, cos]])
    inv = np.block([[cos, sin], [-sin, cos]])
    order = np.concatenate(
        [part * width + h * half + np.arange(half) for h in range(2) for part in range(2)]
    )
    inv = inv[:, order]
    first = np.concatenate([np.cos(outer), -np.sin(outer)], axis=0)
    last = np.concatenate([np.cos(outer).T, -np.sin(outer).T], axis=1) / total
    first_hi, first_lo = split_np(first)
    last_hi, last_lo = split_np(last)
    fwd_hi, fwd_lo = split_np(fwd)
    inv_hi, inv_lo = split_np(inv)
    return (
        np.concatenate([first_hi, first_lo], axis=1),
        np.cos(twist).astype(np.float32),
        (-np.sin(twist)).astype(np.float32),
        fwd_hi,
        fwd_lo,
        inv_hi,
        inv_lo,
        np.concatenate([last_hi, last_lo, last_hi], axis=1),
    )


def split(x):
    high = x.astype(BF)
    return high, (x - high.astype(F32)).astype(BF)


def mm(a, b):
    return jnp.dot(a, b, preferred_element_type=F32)


def kernel(*refs):
    hbm = refs[:14]
    out_ref = refs[14]
    vm = refs[15:29]
    (send_f, send_p, recv_f, recv_p, ret_s, ret_r, stage, z_hi, z_lo, p_hi, p_lo, spec,
     gated, mine, sib_s, sib_r, cross_s, cross_r,
     local_sem, fwd_send, fwd_recv, ret_send, ret_recv, pair_send, pair_recv) = refs[29:]
    filt, keys, vals, first, wre, wim, fwd_hi, fwd_lo, inv_hi, inv_lo, last, quer, skip, weight = vm

    me = lax.axis_index("seq")
    col = lax.axis_index("fsdp")
    n = send_f.shape[0]
    chans = send_f.shape[2]
    tok = keys.shape[0]
    half = tok // 2
    width = keys.shape[1]
    cols = out_ref.shape[1]
    block = min(128, width)
    peers = block // chans
    sibling = col + 1 - 2 * (col % 2)
    across = (col + 2) % 4
    beyond = (sibling + 2) % 4

    loads = [pltpu.make_async_copy(hbm[i], vm[i], local_sem.at[i]) for i in range(14)]
    for copy in loads:
        copy.start()

    barrier = pltpu.get_barrier_semaphore()

    def greet(i, carry):
        pl.semaphore_signal(
            barrier, inc=1, device_id={"seq": (me + i) % n}, device_id_type=MESH
        )
        return carry

    for other in (sibling, across):
        pl.semaphore_signal(barrier, inc=1, device_id={"fsdp": other}, device_id_type=MESH)
    lax.fori_loop(1, n, greet, 0)

    def spread(src, dst, send_sem, recv_sem):
        def go(i, carry):
            peer = (me + i) % n
            pltpu.make_async_remote_copy(
                src_ref=src.at[peer],
                dst_ref=dst.at[me],
                send_sem=send_sem,
                recv_sem=recv_sem,
                device_id={"seq": peer},
                device_id_type=MESH,
            ).start()
            return carry

        lax.fori_loop(1, n, go, 0)
        dst[me] = src[me]

    def landed(buf, sem):
        part = buf.at[pl.ds(0, n - 1)]
        pltpu.make_async_copy(part, part, sem).wait()

    loads[0].wait()
    for h in range(2):
        for j in range(width // block):
            x = filt[h * half:(h + 1) * half, j * block:(j + 1) * block]
            send_f[j * peers:(j + 1) * peers, h] = x.T.astype(BF).reshape(peers, chans, half)
    pl.semaphore_wait(barrier, n + 1)
    spread(send_f, recv_f, fwd_send.at[0], fwd_recv.at[0])
    loads[1].wait()
    loads[2].wait()
    for h in range(2):
        for j in range(width // block):
            rows, lanes = slice(h * half, (h + 1) * half), slice(j * block, (j + 1) * block)
            x = keys[rows, lanes].astype(F32) * vals[rows, lanes].astype(F32)
            send_p[j * peers:(j + 1) * peers, h] = x.T.astype(BF).reshape(peers, chans, half)
    spread(send_p, recv_p, fwd_send.at[1], fwd_recv.at[1])
    for i in range(3, 11):
        loads[i].wait()

    def forward(recv, sink):
        for h in range(2):
            stage[h] = recv[:, h].reshape(n * chans, half).astype(F32)
        for g in range(chans // GROUP):
            for cc in range(GROUP):
                c = g * GROUP + cc
                rows = slice(c * n, (c + 1) * n)
                for h in range(2):
                    lanes = slice(h * half, (h + 1) * half)
                    imag_lanes = slice(tok + h * half, tok + (h + 1) * half)
                    d = stage[h, pl.ds(c, n, stride=chans), :].astype(BF)
                    x = mm(first[...], jnp.concatenate([d, d], axis=0))
                    re, im = x[:n], x[n:]
                    wr, wi = wre[:, lanes], wim[:, lanes]
                    z_hi[rows, lanes], z_lo[rows, lanes] = split(re * wr - im * wi)
                    z_hi[rows, imag_lanes], z_lo[rows, imag_lanes] = split(re * wi + im * wr)
            rows = slice(g * GROUP * n, (g + 1) * GROUP * n)
            high, low = z_hi[rows], z_lo[rows]
            x = mm(high, fwd_hi[...]) + mm(low, fwd_hi[...]) + mm(high, fwd_lo[...])
            sink(rows, x)

    def keep(rows, x):
        spec[rows] = x

    def multiply(rows, x):
        xr, xi = x[:, :tok], x[:, tok:]
        hr, hi = spec[rows, :tok], spec[rows, tok:]
        p_hi[rows, :tok], p_lo[rows, :tok] = split(xr * hr - xi * hi)
        p_hi[rows, tok:], p_lo[rows, tok:] = split(xr * hi + xi * hr)

    landed(recv_f, fwd_recv.at[0])
    forward(recv_f, keep)
    landed(recv_p, fwd_recv.at[1])
    forward(recv_p, multiply)

    for h in range(2):
        lanes = slice(h * half, (h + 1) * half)
        sub = slice(h * tok, (h + 1) * tok)
        for g in range(chans // GROUP):
            rows = slice(g * GROUP * n, (g + 1) * GROUP * n)
            high, low = p_hi[rows], p_lo[rows]
            u = mm(high, inv_hi[:, sub]) + mm(low, inv_hi[:, sub]) + mm(high, inv_lo[:, sub])
            for cc in range(GROUP):
                c = g * GROUP + cc
                ur, ui = u[cc * n:(cc + 1) * n, :half], u[cc * n:(cc + 1) * n, half:]
                wr, wi = wre[:, lanes], wim[:, lanes]
                v = jnp.concatenate([ur * wr + ui * wi, ui * wr - ur * wi], axis=0)
                v_hi, v_lo = split(v)
                stage[h, pl.ds(c, n, stride=chans), :] = mm(
                    last[...], jnp.concatenate([v_hi, v_hi, v_lo], axis=0)
                )
        ret_s[h] = stage[h].astype(BF).reshape(n, chans, half)
        spread(ret_s.at[h], ret_r.at[h], ret_send.at[h], ret_recv.at[h])

    for i in range(11, 14):
        loads[i].wait()

    def partial(owner, tile):
        start = pl.multiple_of(owner * cols + tile * step, step)
        return mm(gated[...], weight[:, pl.ds(start, step)])

    step = min(256, cols)
    tiles = cols // step

    def pair(slot, h, src, dst, target):
        return pltpu.make_async_remote_copy(
            src_ref=src,
            dst_ref=dst,
            send_sem=pair_send.at[slot, h],
            recv_sem=pair_recv.at[slot, h],
            device_id={"fsdp": target},
            device_id_type=MESH,
        )

    def each_tile(body):
        @pl.loop(0, tiles)
        def _(t):
            body(t, pl.ds(pl.multiple_of(t * step, step), step))

    for h in range(2):
        rows = slice(h * half, (h + 1) * half)
        landed(ret_r.at[h], ret_recv.at[h])
        for j in range(width // block):
            lanes = slice(j * block, (j + 1) * block)
            conv = ret_r[h, j * peers:(j + 1) * peers].reshape(block, half).astype(F32).T
            product = keys[rows, lanes].astype(F32) * vals[rows, lanes].astype(F32)
            mixed = conv + skip[:, lanes] * product
            gated[:, lanes] = (quer[rows, lanes].astype(F32) * mixed).astype(BF)

        to_sib = pair(0, h, sib_s.at[0, h], sib_r.at[0, h], sibling)
        to_cross = pair(1, h, cross_s.at[h], cross_r.at[h], across)
        own_sib = pair(2, h, sib_s.at[1, h], sib_r.at[1, h], sibling)

        def far(t, at):
            sib_s[0, h, :, at] = partial(beyond, t).astype(BF)

        def near(t, at):
            mine[:, at] = partial(across, t)

        def sum_up(t, at):
            cross_s[h, :, at] = (mine[:, at] + sib_r[0, h, :, at].astype(F32)).astype(BF)

        def close(t, at):
            sib_s[1, h, :, at] = partial(sibling, t).astype(BF)

        def home(t, at):
            mine[:, at] = partial(col, t)

        def finish(t, at):
            out_ref[rows, at] = (
                mine[:, at] + sib_r[1, h, :, at].astype(F32) + cross_r[h, :, at].astype(F32)
            ).astype(BF)

        each_tile(far)
        to_sib.start()
        each_tile(near)
        to_sib.wait_recv()
        each_tile(sum_up)
        to_cross.start()
        each_tile(close)
        own_sib.start()
        each_tile(home)
        own_sib.wait_recv()
        to_cross.wait_recv()
        each_tile(finish)
        to_sib.wait_send()
        own_sib.wait_send()
        to_cross.wait_send()

    landed(send_f, fwd_send.at[0])
    landed(send_p, fwd_send.at[1])
    landed(ret_s.at[0], ret_send.at[0])
    landed(ret_s.at[1], ret_send.at[1])


def body(queries, keys, values, filters, skip_weight, out_weight):
    n = lax.axis_size("seq")
    tok, width = keys.shape
    cols = width
    half = tok // 2
    chans = width // n
    tables = make_tables(n, tok)
    first, wre, wim, fwd_hi, fwd_lo, inv_hi, inv_lo, last = [jnp.asarray(t) for t in tables]
    operands = (
        filters, keys, values, first, wre, wim, fwd_hi, fwd_lo, inv_hi, inv_lo, last,
        queries, skip_weight.reshape(1, width), out_weight,
    )
    dma = pltpu.SemaphoreType.DMA
    scratch = [pltpu.VMEM(x.shape, x.dtype) for x in operands] + [
        pltpu.VMEM((n, 2, chans, half), BF),
        pltpu.VMEM((n, 2, chans, half), BF),
        pltpu.VMEM((n, 2, chans, half), BF),
        pltpu.VMEM((n, 2, chans, half), BF),
        pltpu.VMEM((2, n, chans, half), BF),
        pltpu.VMEM((2, n, chans, half), BF),
        pltpu.VMEM((2, n * chans, half), F32),
        pltpu.VMEM((n * chans, 2 * tok), BF),
        pltpu.VMEM((n * chans, 2 * tok), BF),
        pltpu.VMEM((n * chans, 2 * tok), BF),
        pltpu.VMEM((n * chans, 2 * tok), BF),
        pltpu.VMEM((n * chans, 2 * tok), F32),
        pltpu.VMEM((half, width), BF),
        pltpu.VMEM((half, cols), F32),
        pltpu.VMEM((2, 2, half, cols), BF),
        pltpu.VMEM((2, 2, half, cols), BF),
        pltpu.VMEM((2, half, cols), BF),
        pltpu.VMEM((2, half, cols), BF),
        dma((14,)),
        dma((2,)),
        dma((2,)),
        dma((2,)),
        dma((2,)),
        dma((3, 2)),
        dma((3, 2)),
    ]
    flops = 2 * chans * n * 3 * (2 * tok) * (2 * tok) * 3 + 2 * tok * width * 4 * cols
    return pl.pallas_call(
        kernel,
        out_shape=jax.ShapeDtypeStruct((tok, cols), BF),
        in_specs=[pl.BlockSpec(memory_space=pl.ANY)] * len(operands),
        out_specs=pl.BlockSpec(memory_space=pltpu.VMEM),
        scratch_shapes=scratch,
        compiler_params=pltpu.CompilerParams(
            collective_id=0, has_side_effects=True, vmem_limit_bytes=48 * 1024 * 1024
        ),
        cost_estimate=pl.CostEstimate(
            flops=flops, bytes_accessed=16 * 1024 * 1024, transcendentals=0
        ),
        name="hyena",
    )(*operands)


def solution(mesh):
    in_specs = (
        P("seq", "fsdp"),
        P("seq", "fsdp"),
        P("seq", "fsdp"),
        P("seq", "fsdp"),
        P("fsdp"),
        P("fsdp", None),
    )
    out_specs = P("seq", "fsdp")
    return jax.shard_map(body, mesh=mesh, in_specs=in_specs, out_specs=out_specs, check_vma=False)
```

```python
import functools
import math

import jax
import jax.numpy as jnp
import ml_dtypes
import numpy as np
from jax import lax
from jax.experimental import pallas as pl
from jax.experimental.pallas import tpu as pltpu
from jax.sharding import PartitionSpec as P

MESH = pl.DeviceIdType.MESH
BF = jnp.bfloat16
F32 = jnp.float32
GROUP = 4


def split_np(table):
    high = table.astype(np.float32).astype(ml_dtypes.bfloat16)
    low = (table - high.astype(np.float64)).astype(np.float32).astype(ml_dtypes.bfloat16)
    return high, low


def make_tables(n_blocks, width):
    half = width // 2
    total = n_blocks * width
    theta = np.arange(n_blocks) + 0.25
    blocks = np.arange(n_blocks)
    lanes = np.arange(width)
    outer = 2 * math.pi * np.outer(theta, blocks) / n_blocks
    twist = 2 * math.pi * np.outer(theta, lanes) / total
    inner = 2 * math.pi * (np.outer(lanes, lanes) % width) / width
    cos, sin = np.cos(inner), np.sin(inner)
    fwd = np.block([[cos, -sin], [sin, cos]])
    inv = np.block([[cos, sin], [-sin, cos]])
    order = np.concatenate(
        [part * width + h * half + np.arange(half) for h in range(2) for part in range(2)]
    )
    inv = inv[:, order]
    first = np.concatenate([np.cos(outer), -np.sin(outer)], axis=0)
    last = np.concatenate([np.cos(outer).T, -np.sin(outer).T], axis=1) / total
    first_hi, first_lo = split_np(first)
    last_hi, last_lo = split_np(last)
    fwd_hi, fwd_lo = split_np(fwd)
    inv_hi, inv_lo = split_np(inv)
    return (
        np.concatenate([first_hi, first_lo], axis=1),
        np.cos(twist).astype(np.float32),
        (-np.sin(twist)).astype(np.float32),
        fwd_hi,
        fwd_lo,
        inv_hi,
        inv_lo,
        np.concatenate([last_hi, last_lo, last_hi], axis=1),
    )


def split(x):
    high = x.astype(BF)
    return high, (x - high.astype(F32)).astype(BF)


def mm(a, b):
    return jnp.dot(a, b, preferred_element_type=F32)


def kernel(*refs):
    hbm = refs[:14]
    out_ref = refs[14]
    vm = refs[15:29]
    (send_f, send_p, recv_f, recv_p, ret_s, ret_r, stage, z_hi, z_lo, p_hi, p_lo, spec,
     gated, mine, sib_s, sib_r, cross_s, cross_r,
     local_sem, fwd_send, fwd_recv, ret_send, ret_recv, pair_send, pair_recv) = refs[29:]
    filt, keys, vals, first, wre, wim, fwd_hi, fwd_lo, inv_hi, inv_lo, last, quer, skip, weight = vm

    me = lax.axis_index("seq")
    col = lax.axis_index("fsdp")
    n = send_f.shape[0]
    chans = send_f.shape[2]
    tok = keys.shape[0]
    half = tok // 2
    width = keys.shape[1]
    cols = out_ref.shape[1]
    block = min(128, width)
    peers = block // chans
    sibling = col + 1 - 2 * (col % 2)
    across = (col + 2) % 4
    beyond = (sibling + 2) % 4

    loads = [pltpu.make_async_copy(hbm[i], vm[i], local_sem.at[i]) for i in range(14)]
    for copy in loads:
        copy.start()

    barrier = pltpu.get_barrier_semaphore()

    def greet(i, carry):
        pl.semaphore_signal(
            barrier, inc=1, device_id={"seq": (me + i) % n}, device_id_type=MESH
        )
        return carry

    for other in (sibling, across):
        pl.semaphore_signal(barrier, inc=1, device_id={"fsdp": other}, device_id_type=MESH)
    lax.fori_loop(1, n, greet, 0)

    def spread(src, dst, send_sem, recv_sem):
        def go(i, carry):
            peer = (me + i) % n
            pltpu.make_async_remote_copy(
                src_ref=src.at[peer],
                dst_ref=dst.at[me],
                send_sem=send_sem,
                recv_sem=recv_sem,
                device_id={"seq": peer},
                device_id_type=MESH,
            ).start()
            return carry

        lax.fori_loop(1, n, go, 0)
        dst[me] = src[me]

    def landed(buf, sem):
        part = buf.at[pl.ds(0, n - 1)]
        pltpu.make_async_copy(part, part, sem).wait()

    loads[0].wait()
    for h in range(2):
        for j in range(width // block):
            x = filt[h * half:(h + 1) * half, j * block:(j + 1) * block]
            send_f[j * peers:(j + 1) * peers, h] = x.T.astype(BF).reshape(peers, chans, half)
    pl.semaphore_wait(barrier, n + 1)
    spread(send_f, recv_f, fwd_send.at[0], fwd_recv.at[0])
    loads[1].wait()
    loads[2].wait()
    for h in range(2):
        for j in range(width // block):
            rows, lanes = slice(h * half, (h + 1) * half), slice(j * block, (j + 1) * block)
            x = keys[rows, lanes].astype(F32) * vals[rows, lanes].astype(F32)
            send_p[j * peers:(j + 1) * peers, h] = x.T.astype(BF).reshape(peers, chans, half)
    spread(send_p, recv_p, fwd_send.at[1], fwd_recv.at[1])
    for i in range(3, 11):
        loads[i].wait()

    def forward(recv, sink):
        for h in range(2):
            stage[h] = recv[:, h].reshape(n * chans, half).astype(F32)
        for g in range(chans // GROUP):
            for cc in range(GROUP):
                c = g * GROUP + cc
                rows = slice(c * n, (c + 1) * n)
                for h in range(2):
                    lanes = slice(h * half, (h + 1) * half)
                    imag_lanes = slice(tok + h * half, tok + (h + 1) * half)
                    d = stage[h, pl.ds(c, n, stride=chans), :].astype(BF)
                    x = mm(first[...], jnp.concatenate([d, d], axis=0))
                    re, im = x[:n], x[n:]
                    wr, wi = wre[:, lanes], wim[:, lanes]
                    z_hi[rows, lanes], z_lo[rows, lanes] = split(re * wr - im * wi)
                    z_hi[rows, imag_lanes], z_lo[rows, imag_lanes] = split(re * wi + im * wr)
            rows = slice(g * GROUP * n, (g + 1) * GROUP * n)
            high, low = z_hi[rows], z_lo[rows]
            x = mm(high, fwd_hi[...]) + mm(low, fwd_hi[...]) + mm(high, fwd_lo[...])
            sink(rows, x)

    def keep(rows, x):
        spec[rows] = x

    def multiply(rows, x):
        xr, xi = x[:, :tok], x[:, tok:]
        hr, hi = spec[rows, :tok], spec[rows, tok:]
        p_hi[rows, :tok], p_lo[rows, :tok] = split(xr * hr - xi * hi)
        p_hi[rows, tok:], p_lo[rows, tok:] = split(xr * hi + xi * hr)

    landed(recv_f, fwd_recv.at[0])
    forward(recv_f, keep)
    landed(recv_p, fwd_recv.at[1])
    forward(recv_p, multiply)

    for h in range(2):
        lanes = slice(h * half, (h + 1) * half)
        sub = slice(h * tok, (h + 1) * tok)
        for g in range(chans // GROUP):
            rows = slice(g * GROUP * n, (g + 1) * GROUP * n)
            high, low = p_hi[rows], p_lo[rows]
            u = mm(high, inv_hi[:, sub]) + mm(low, inv_hi[:, sub]) + mm(high, inv_lo[:, sub])
            for cc in range(GROUP):
                c = g * GROUP + cc
                ur, ui = u[cc * n:(cc + 1) * n, :half], u[cc * n:(cc + 1) * n, half:]
                wr, wi = wre[:, lanes], wim[:, lanes]
                v = jnp.concatenate([ur * wr + ui * wi, ui * wr - ur * wi], axis=0)
                v_hi, v_lo = split(v)
                stage[h, pl.ds(c, n, stride=chans), :] = mm(
                    last[...], jnp.concatenate([v_hi, v_hi, v_lo], axis=0)
                )
        ret_s[h] = stage[h].astype(BF).reshape(n, chans, half)
        spread(ret_s.at[h], ret_r.at[h], ret_send.at[h], ret_recv.at[h])

    for i in range(11, 14):
        loads[i].wait()

    def partial(owner, tile):
        start = pl.multiple_of(owner * cols + tile * step, step)
        return mm(gated[...], weight[:, pl.ds(start, step)])

    step = min(256, cols)
    tiles = cols // step

    def pair(slot, h, src, dst, target):
        return pltpu.make_async_remote_copy(
            src_ref=src,
            dst_ref=dst,
            send_sem=pair_send.at[slot, h],
            recv_sem=pair_recv.at[slot, h],
            device_id={"fsdp": target},
            device_id_type=MESH,
        )

    def each_tile(body):
        @pl.loop(0, tiles)
        def _(t):
            body(t, pl.ds(pl.multiple_of(t * step, step), step))

    for h in range(2):
        rows = slice(h * half, (h + 1) * half)
        landed(ret_r.at[h], ret_recv.at[h])
        for j in range(width // block):
            lanes = slice(j * block, (j + 1) * block)
            conv = ret_r[h, j * peers:(j + 1) * peers].reshape(block, half).astype(F32).T
            product = keys[rows, lanes].astype(F32) * vals[rows, lanes].astype(F32)
            mixed = conv + skip[:, lanes] * product
            gated[:, lanes] = (quer[rows, lanes].astype(F32) * mixed).astype(BF)

        to_sib = pair(0, h, sib_s.at[0, h], sib_r.at[0, h], sibling)
        to_cross = pair(1, h, cross_s.at[h], cross_r.at[h], across)
        own_sib = pair(2, h, sib_s.at[1, h], sib_r.at[1, h], sibling)

        def far(t, at):
            sib_s[0, h, :, at] = partial(beyond, t).astype(BF)

        def near(t, at):
            mine[:, at] = partial(across, t)

        def sum_up(t, at):
            cross_s[h, :, at] = (mine[:, at] + sib_r[0, h, :, at].astype(F32)).astype(BF)

        def close(t, at):
            sib_s[1, h, :, at] = partial(sibling, t).astype(BF)

        def home(t, at):
            mine[:, at] = partial(col, t)

        def finish(t, at):
            out_ref[rows, at] = (
                mine[:, at] + sib_r[1, h, :, at].astype(F32) + cross_r[h, :, at].astype(F32)
            ).astype(BF)

        each_tile(far)
        to_sib.start()
        each_tile(near)
        to_sib.wait_recv()
        each_tile(sum_up)
        to_cross.start()
        each_tile(close)
        own_sib.start()
        each_tile(home)
        own_sib.wait_recv()
        to_cross.wait_recv()
        each_tile(finish)
        to_sib.wait_send()
        own_sib.wait_send()
        to_cross.wait_send()

    landed(send_f, fwd_send.at[0])
    landed(send_p, fwd_send.at[1])
    landed(ret_s.at[0], ret_send.at[0])
    landed(ret_s.at[1], ret_send.at[1])


def body(queries, keys, values, filters, skip_weight, out_weight):
    n = lax.axis_size("seq")
    tok, width = keys.shape
    cols = width
    half = tok // 2
    chans = width // n
    tables = make_tables(n, tok)
    first, wre, wim, fwd_hi, fwd_lo, inv_hi, inv_lo, last = [jnp.asarray(t) for t in tables]
    operands = (
        filters, keys, values, first, wre, wim, fwd_hi, fwd_lo, inv_hi, inv_lo, last,
        queries, skip_weight.reshape(1, width), out_weight,
    )
    dma = pltpu.SemaphoreType.DMA
    scratch = [pltpu.VMEM(x.shape, x.dtype) for x in operands] + [
        pltpu.VMEM((n, 2, chans, half), BF),
        pltpu.VMEM((n, 2, chans, half), BF),
        pltpu.VMEM((n, 2, chans, half), BF),
        pltpu.VMEM((n, 2, chans, half), BF),
        pltpu.VMEM((2, n, chans, half), BF),
        pltpu.VMEM((2, n, chans, half), BF),
        pltpu.VMEM((2, n * chans, half), F32),
        pltpu.VMEM((n * chans, 2 * tok), BF),
        pltpu.VMEM((n * chans, 2 * tok), BF),
        pltpu.VMEM((n * chans, 2 * tok), BF),
        pltpu.VMEM((n * chans, 2 * tok), BF),
        pltpu.VMEM((n * chans, 2 * tok), F32),
        pltpu.VMEM((half, width), BF),
        pltpu.VMEM((half, cols), F32),
        pltpu.VMEM((2, 2, half, cols), BF),
        pltpu.VMEM((2, 2, half, cols), BF),
        pltpu.VMEM((2, half, cols), BF),
        pltpu.VMEM((2, half, cols), BF),
        dma((14,)),
        dma((2,)),
        dma((2,)),
        dma((2,)),
        dma((2,)),
        dma((3, 2)),
        dma((3, 2)),
    ]
    flops = 2 * chans * n * 3 * (2 * tok) * (2 * tok) * 3 + 2 * tok * width * 4 * cols
    return pl.pallas_call(
        kernel,
        out_shape=jax.ShapeDtypeStruct((tok, cols), BF),
        in_specs=[pl.BlockSpec(memory_space=pl.ANY)] * len(operands),
        out_specs=pl.BlockSpec(memory_space=pltpu.VMEM),
        scratch_shapes=scratch,
        compiler_params=pltpu.CompilerParams(
            collective_id=0, has_side_effects=True, vmem_limit_bytes=62 * 1024 * 1024
        ),
        cost_estimate=pl.CostEstimate(
            flops=flops, bytes_accessed=16 * 1024 * 1024, transcendentals=0
        ),
        name="hyena",
    )(*operands)


def solution(mesh):
    in_specs = (
        P("seq", "fsdp"),
        P("seq", "fsdp"),
        P("seq", "fsdp"),
        P("seq", "fsdp"),
        P("fsdp"),
        P("fsdp", None),
    )
    out_specs = P("seq", "fsdp")
    return jax.shard_map(body, mesh=mesh, in_specs=in_specs, out_specs=out_specs, check_vma=False)
```

```python
import functools
import math

import jax
import jax.numpy as jnp
import ml_dtypes
import numpy as np
from jax import lax
from jax.experimental import pallas as pl
from jax.experimental.pallas import tpu as pltpu
from jax.sharding import PartitionSpec as P

MESH = pl.DeviceIdType.MESH
BF = jnp.bfloat16
F32 = jnp.float32
GROUP = 4
PARTS = 2


def split_np(table):
    high = table.astype(np.float32).astype(ml_dtypes.bfloat16)
    low = (table - high.astype(np.float64)).astype(np.float32).astype(ml_dtypes.bfloat16)
    return high, low


def make_tables(n_blocks, width):
    half = width // 2
    total = n_blocks * width
    theta = np.arange(n_blocks) + 0.25
    blocks = np.arange(n_blocks)
    lanes = np.arange(width)
    outer = 2 * math.pi * np.outer(theta, blocks) / n_blocks
    twist = 2 * math.pi * np.outer(theta, lanes) / total
    inner = 2 * math.pi * (np.outer(lanes, lanes) % width) / width
    cos, sin = np.cos(inner), np.sin(inner)
    fwd = np.block([[cos, -sin], [sin, cos]])
    inv = np.block([[cos, sin], [-sin, cos]])
    order = np.concatenate(
        [part * width + h * half + np.arange(half) for h in range(2) for part in range(2)]
    )
    inv = inv[:, order]
    first = np.concatenate([np.cos(outer), -np.sin(outer)], axis=0)
    last = np.concatenate([np.cos(outer).T, -np.sin(outer).T], axis=1) / total
    first_hi, first_lo = split_np(first)
    last_hi, last_lo = split_np(last)
    fwd_hi, fwd_lo = split_np(fwd)
    inv_hi, inv_lo = split_np(inv)
    return (
        np.concatenate([first_hi, first_lo], axis=1),
        np.cos(twist).astype(np.float32),
        (-np.sin(twist)).astype(np.float32),
        fwd_hi,
        fwd_lo,
        inv_hi,
        inv_lo,
        np.concatenate([last_hi, last_lo, last_hi], axis=1),
    )


def split(x):
    high = x.astype(BF)
    return high, (x - high.astype(F32)).astype(BF)


def mm(a, b):
    return jnp.dot(a, b, preferred_element_type=F32)


def kernel(*refs):
    hbm = refs[:14]
    out_ref = refs[14]
    vm = refs[15:29]
    (send_f, send_p, recv_f, recv_p, ret_s, ret_r, stage, z_hi, z_lo, p_hi, p_lo, spec,
     gated, mine, sib_s, sib_r, own_s, own_r, cross_s, cross_r,
     local_sem, fwd_send, fwd_recv, ret_send, ret_recv, pair_send, pair_recv) = refs[29:]
    filt, keys, vals, first, wre, wim, fwd_hi, fwd_lo, inv_hi, inv_lo, last, quer, skip, weight = vm

    me = lax.axis_index("seq")
    col = lax.axis_index("fsdp")
    n = send_f.shape[0]
    chans = send_f.shape[2]
    tok = keys.shape[0]
    half = tok // 2
    width = keys.shape[1]
    cols = out_ref.shape[1]
    block = min(128, width)
    peers = block // chans
    sibling = col + 1 - 2 * (col % 2)
    across = (col + 2) % 4
    beyond = (sibling + 2) % 4

    loads = [pltpu.make_async_copy(hbm[i], vm[i], local_sem.at[i]) for i in range(14)]
    for copy in loads:
        copy.start()

    barrier = pltpu.get_barrier_semaphore()

    def greet(i, carry):
        pl.semaphore_signal(
            barrier, inc=1, device_id={"seq": (me + i) % n}, device_id_type=MESH
        )
        return carry

    for other in (sibling, across):
        pl.semaphore_signal(barrier, inc=1, device_id={"fsdp": other}, device_id_type=MESH)
    lax.fori_loop(1, n, greet, 0)

    def spread(src, dst, send_sem, recv_sem):
        def go(i, carry):
            peer = (me + i) % n
            pltpu.make_async_remote_copy(
                src_ref=src.at[peer],
                dst_ref=dst.at[me],
                send_sem=send_sem,
                recv_sem=recv_sem,
                device_id={"seq": peer},
                device_id_type=MESH,
            ).start()
            return carry

        lax.fori_loop(1, n, go, 0)
        dst[me] = src[me]

    def landed(buf, sem):
        part = buf.at[pl.ds(0, n - 1)]
        pltpu.make_async_copy(part, part, sem).wait()

    loads[0].wait()
    for h in range(2):
        for j in range(width // block):
            x = filt[h * half:(h + 1) * half, j * block:(j + 1) * block]
            send_f[j * peers:(j + 1) * peers, h] = x.T.astype(BF).reshape(peers, chans, half)
    pl.semaphore_wait(barrier, n + 1)
    spread(send_f, recv_f, fwd_send.at[0], fwd_recv.at[0])
    loads[1].wait()
    loads[2].wait()
    for h in range(2):
        for j in range(width // block):
            rows, lanes = slice(h * half, (h + 1) * half), slice(j * block, (j + 1) * block)
            x = keys[rows, lanes].astype(F32) * vals[rows, lanes].astype(F32)
            send_p[j * peers:(j + 1) * peers, h] = x.T.astype(BF).reshape(peers, chans, half)
    spread(send_p, recv_p, fwd_send.at[1], fwd_recv.at[1])
    for i in range(3, 11):
        loads[i].wait()

    def forward(recv, sink):
        for h in range(2):
            stage[h] = recv[:, h].reshape(n * chans, half).astype(F32)
        for g in range(chans // GROUP):
            for cc in range(GROUP):
                c = g * GROUP + cc
                rows = slice(c * n, (c + 1) * n)
                for h in range(2):
                    lanes = slice(h * half, (h + 1) * half)
                    imag_lanes = slice(tok + h * half, tok + (h + 1) * half)
                    d = stage[h, pl.ds(c, n, stride=chans), :].astype(BF)
                    x = mm(first[...], jnp.concatenate([d, d], axis=0))
                    re, im = x[:n], x[n:]
                    wr, wi = wre[:, lanes], wim[:, lanes]
                    z_hi[rows, lanes], z_lo[rows, lanes] = split(re * wr - im * wi)
                    z_hi[rows, imag_lanes], z_lo[rows, imag_lanes] = split(re * wi + im * wr)
            rows = slice(g * GROUP * n, (g + 1) * GROUP * n)
            high, low = z_hi[rows], z_lo[rows]
            x = mm(high, fwd_hi[...]) + mm(low, fwd_hi[...]) + mm(high, fwd_lo[...])
            sink(rows, x)

    def keep(rows, x):
        spec[rows] = x

    def multiply(rows, x):
        xr, xi = x[:, :tok], x[:, tok:]
        hr, hi = spec[rows, :tok], spec[rows, tok:]
        p_hi[rows, :tok], p_lo[rows, :tok] = split(xr * hr - xi * hi)
        p_hi[rows, tok:], p_lo[rows, tok:] = split(xr * hi + xi * hr)

    landed(recv_f, fwd_recv.at[0])
    forward(recv_f, keep)
    landed(recv_p, fwd_recv.at[1])
    forward(recv_p, multiply)

    for h in range(2):
        lanes = slice(h * half, (h + 1) * half)
        sub = slice(h * tok, (h + 1) * tok)
        for g in range(chans // GROUP):
            rows = slice(g * GROUP * n, (g + 1) * GROUP * n)
            high, low = p_hi[rows], p_lo[rows]
            u = mm(high, inv_hi[:, sub]) + mm(low, inv_hi[:, sub]) + mm(high, inv_lo[:, sub])
            for cc in range(GROUP):
                c = g * GROUP + cc
                ur, ui = u[cc * n:(cc + 1) * n, :half], u[cc * n:(cc + 1) * n, half:]
                wr, wi = wre[:, lanes], wim[:, lanes]
                v = jnp.concatenate([ur * wr + ui * wi, ui * wr - ur * wi], axis=0)
                v_hi, v_lo = split(v)
                stage[h, pl.ds(c, n, stride=chans), :] = mm(
                    last[...], jnp.concatenate([v_hi, v_hi, v_lo], axis=0)
                )
        ret_s[h] = stage[h].astype(BF).reshape(n, chans, half)
        spread(ret_s.at[h], ret_r.at[h], ret_send.at[h], ret_recv.at[h])

    for i in range(11, 14):
        loads[i].wait()

    part = cols // PARTS

    def pair(slot, h, src, dst, target):
        return pltpu.make_async_remote_copy(
            src_ref=src,
            dst_ref=dst,
            send_sem=pair_send.at[slot, h],
            recv_sem=pair_recv.at[slot, h],
            device_id={"fsdp": target},
            device_id_type=MESH,
        )

    def partial(h, owner, piece):
        start = pl.multiple_of(owner * cols + piece * part, part)
        return mm(gated[h], weight[:, pl.ds(start, part)])

    def to_sib(h, piece):
        return pair(piece, h, sib_s.at[h, piece], sib_r.at[h, piece], sibling)

    def to_cross(h, piece):
        return pair(PARTS + piece, h, cross_s.at[h, piece], cross_r.at[h, piece], across)

    def own_sib(h, piece):
        return pair(2 * PARTS + piece, h, own_s.at[h, piece], own_r.at[h, piece], sibling)

    def gate(h):
        rows = slice(h * half, (h + 1) * half)
        for j in range(width // block):
            lanes = slice(j * block, (j + 1) * block)
            conv = ret_r[h, j * peers:(j + 1) * peers].reshape(block, half).astype(F32).T
            product = keys[rows, lanes].astype(F32) * vals[rows, lanes].astype(F32)
            mixed = conv + skip[:, lanes] * product
            gated[h, :, lanes] = (quer[rows, lanes].astype(F32) * mixed).astype(BF)

    def leave(h):
        for piece in range(PARTS):
            sib_s[h, piece] = partial(h, beyond, piece).astype(BF)
            to_sib(h, piece).start()
        for piece in range(PARTS):
            near = partial(h, across, piece)
            to_sib(h, piece).wait_recv()
            cross_s[h, piece] = (near + sib_r[h, piece].astype(F32)).astype(BF)
            to_cross(h, piece).start()

    def stay(h):
        for piece in range(PARTS):
            own_s[h, piece] = partial(h, sibling, piece).astype(BF)
            own_sib(h, piece).start()
        for piece in range(PARTS):
            mine[h, piece] = partial(h, col, piece)

    def finish(h):
        rows = slice(h * half, (h + 1) * half)
        for piece in range(PARTS):
            own_sib(h, piece).wait_recv()
            to_cross(h, piece).wait_recv()
            out_ref[rows, piece * part:(piece + 1) * part] = (
                mine[h, piece] + own_r[h, piece].astype(F32) + cross_r[h, piece].astype(F32)
            ).astype(BF)

    landed(ret_r.at[0], ret_recv.at[0])
    gate(0)
    leave(0)
    stay(0)
    landed(ret_r.at[1], ret_recv.at[1])
    gate(1)
    leave(1)
    stay(1)
    finish(0)
    finish(1)
    for h in range(2):
        for piece in range(PARTS):
            to_sib(h, piece).wait_send()
            to_cross(h, piece).wait_send()
            own_sib(h, piece).wait_send()
    landed(send_f, fwd_send.at[0])
    landed(send_p, fwd_send.at[1])
    landed(ret_s.at[0], ret_send.at[0])
    landed(ret_s.at[1], ret_send.at[1])


def body(queries, keys, values, filters, skip_weight, out_weight):
    n = lax.axis_size("seq")
    tok, width = keys.shape
    cols = width
    half = tok // 2
    chans = width // n
    tables = make_tables(n, tok)
    first, wre, wim, fwd_hi, fwd_lo, inv_hi, inv_lo, last = [jnp.asarray(t) for t in tables]
    operands = (
        filters, keys, values, first, wre, wim, fwd_hi, fwd_lo, inv_hi, inv_lo, last,
        queries, skip_weight.reshape(1, width), out_weight,
    )
    dma = pltpu.SemaphoreType.DMA
    scratch = [pltpu.VMEM(x.shape, x.dtype) for x in operands] + [
        pltpu.VMEM((n, 2, chans, half), BF),
        pltpu.VMEM((n, 2, chans, half), BF),
        pltpu.VMEM((n, 2, chans, half), BF),
        pltpu.VMEM((n, 2, chans, half), BF),
        pltpu.VMEM((2, n, chans, half), BF),
        pltpu.VMEM((2, n, chans, half), BF),
        pltpu.VMEM((2, n * chans, half), F32),
        pltpu.VMEM((n * chans, 2 * tok), BF),
        pltpu.VMEM((n * chans, 2 * tok), BF),
        pltpu.VMEM((n * chans, 2 * tok), BF),
        pltpu.VMEM((n * chans, 2 * tok), BF),
        pltpu.VMEM((n * chans, 2 * tok), F32),
        pltpu.VMEM((2, half, width), BF),
        pltpu.VMEM((2, PARTS, half, cols // PARTS), F32),
        pltpu.VMEM((2, PARTS, half, cols // PARTS), BF),
        pltpu.VMEM((2, PARTS, half, cols // PARTS), BF),
        pltpu.VMEM((2, PARTS, half, cols // PARTS), BF),
        pltpu.VMEM((2, PARTS, half, cols // PARTS), BF),
        pltpu.VMEM((2, PARTS, half, cols // PARTS), BF),
        pltpu.VMEM((2, PARTS, half, cols // PARTS), BF),
        dma((14,)),
        dma((2,)),
        dma((2,)),
        dma((2,)),
        dma((2,)),
        dma((3 * PARTS, 2)),
        dma((3 * PARTS, 2)),
    ]
    flops = 2 * chans * n * 3 * (2 * tok) * (2 * tok) * 3 + 2 * tok * width * 4 * cols
    return pl.pallas_call(
        kernel,
        out_shape=jax.ShapeDtypeStruct((tok, cols), BF),
        in_specs=[pl.BlockSpec(memory_space=pl.ANY)] * len(operands),
        out_specs=pl.BlockSpec(memory_space=pltpu.VMEM),
        scratch_shapes=scratch,
        compiler_params=pltpu.CompilerParams(
            collective_id=0, has_side_effects=True, vmem_limit_bytes=62 * 1024 * 1024
        ),
        cost_estimate=pl.CostEstimate(
            flops=flops, bytes_accessed=16 * 1024 * 1024, transcendentals=0
        ),
        name="hyena",
    )(*operands)


def solution(mesh):
    in_specs = (
        P("seq", "fsdp"),
        P("seq", "fsdp"),
        P("seq", "fsdp"),
        P("seq", "fsdp"),
        P("fsdp"),
        P("fsdp", None),
    )
    out_specs = P("seq", "fsdp")
    return jax.shard_map(body, mesh=mesh, in_specs=in_specs, out_specs=out_specs, check_vma=False)
```

```python
import functools
import math

import jax
import jax.numpy as jnp
import ml_dtypes
import numpy as np
from jax import lax
from jax.experimental import pallas as pl
from jax.experimental.pallas import tpu as pltpu
from jax.sharding import PartitionSpec as P

MESH = pl.DeviceIdType.MESH
BF = jnp.bfloat16
F32 = jnp.float32
GROUP = 4
PARTS = 2
CHUNKS = 2


def split_np(table):
    high = table.astype(np.float32).astype(ml_dtypes.bfloat16)
    low = (table - high.astype(np.float64)).astype(np.float32).astype(ml_dtypes.bfloat16)
    return high, low


def make_tables(n_blocks, width):
    half = width // 2
    total = n_blocks * width
    theta = np.arange(n_blocks) + 0.25
    lanes = np.arange(half)
    outer = 2 * math.pi * np.outer(theta, np.arange(n_blocks)) / n_blocks
    twist = 2 * math.pi * np.outer(theta, np.arange(width)) / total
    inner = 2 * math.pi * (np.outer(lanes, lanes) % half) / half
    cos, sin = np.cos(inner), np.sin(inner)
    turn = 2 * math.pi * lanes[None, :] / width
    first = np.concatenate([np.cos(outer), -np.sin(outer)], axis=0)
    last = np.concatenate([np.cos(outer).T, -np.sin(outer).T], axis=1) / total
    first_hi, first_lo = split_np(first)
    last_hi, last_lo = split_np(last)
    return (
        np.concatenate([first_hi, first_lo], axis=1),
        np.cos(twist).astype(np.float32),
        (-np.sin(twist)).astype(np.float32),
        np.cos(turn).astype(np.float32),
        (-np.sin(turn)).astype(np.float32),
        *split_np(np.block([[cos, -sin], [sin, cos]])),
        *split_np(np.block([[cos, sin], [-sin, cos]])),
        np.concatenate([last_hi, last_lo, last_hi], axis=1),
    )


def split(x):
    high = x.astype(BF)
    return high, (x - high.astype(F32)).astype(BF)


def mm(a, b):
    return jnp.dot(a, b, preferred_element_type=F32)


def kernel(*refs):
    hbm = refs[:16]
    out_ref = refs[16]
    vm = refs[17:33]
    (send_f, send_p, recv_f, recv_p, ret_s, ret_r, stage, conv_f, z_hi, z_lo, waves, spec,
     gated, mine, sib_s, sib_r, own_s, own_r, cross_s, cross_r,
     local_sem, fwd_send, fwd_recv, ret_send, ret_recv, pair_send, pair_recv) = refs[33:]
    (filt, keys, vals, first, wre, wim, ure, uim, fwd_hi, fwd_lo, inv_hi, inv_lo, last,
     quer, skip, weight) = vm

    me = lax.axis_index("seq")
    col = lax.axis_index("fsdp")
    n = send_f.shape[0]
    chans = send_f.shape[2]
    tok = keys.shape[0]
    half = tok // 2
    width = keys.shape[1]
    cols = out_ref.shape[1]
    some = chans // CHUNKS
    block = min(128, width)
    peers = block // chans
    sibling = col + 1 - 2 * (col % 2)
    across = (col + 2) % 4
    beyond = (sibling + 2) % 4

    loads = [pltpu.make_async_copy(hbm[i], vm[i], local_sem.at[i]) for i in range(16)]
    for copy in loads[:3]:
        copy.start()

    barrier = pltpu.get_barrier_semaphore()

    def greet(i, carry):
        pl.semaphore_signal(
            barrier, inc=1, device_id={"seq": (me + i) % n}, device_id_type=MESH
        )
        return carry

    for other in (sibling, across):
        pl.semaphore_signal(barrier, inc=1, device_id={"fsdp": other}, device_id_type=MESH)
    lax.fori_loop(1, n, greet, 0)

    def spread(src, dst, send_sem, recv_sem):
        def go(i, carry):
            peer = (me + i) % n
            pltpu.make_async_remote_copy(
                src_ref=src.at[peer],
                dst_ref=dst.at[me],
                send_sem=send_sem,
                recv_sem=recv_sem,
                device_id={"seq": peer},
                device_id_type=MESH,
            ).start()
            return carry

        lax.fori_loop(1, n, go, 0)
        dst[me] = src[me]

    def landed(buf, sem):
        part = buf.at[pl.ds(0, n - 1)]
        pltpu.make_async_copy(part, part, sem).wait()

    loads[0].wait()
    for h in range(2):
        for j in range(width // block):
            x = filt[h * half:(h + 1) * half, j * block:(j + 1) * block]
            send_f[j * peers:(j + 1) * peers, h] = x.T.astype(BF).reshape(peers, chans, half)
    pl.semaphore_wait(barrier, n + 1)
    spread(send_f, recv_f, fwd_send.at[0], fwd_recv.at[0])
    for copy in loads[3:13]:
        copy.start()
    loads[1].wait()
    loads[2].wait()
    for j in range(width // block):
        lanes = slice(j * block, (j + 1) * block)
        turned = []
        for h in range(2):
            rows = slice(h * half, (h + 1) * half)
            x = keys[rows, lanes].astype(F32) * vals[rows, lanes].astype(F32)
            turned.append(x.T.reshape(peers, chans, half))
        for q in range(CHUNKS):
            sub = slice(q * some, (q + 1) * some)
            send_p[q, j * peers:(j + 1) * peers] = jnp.concatenate(
                [x[:, sub] for x in turned], axis=1
            ).astype(BF)
    for q in range(CHUNKS):
        spread(send_p.at[q], recv_p.at[q], fwd_send.at[1 + q], fwd_recv.at[1 + q])
    for copy in loads[13:]:
        copy.start()
    for i in range(3, 13):
        loads[i].wait()

    def rotate(x, y, wr, wi):
        return x * wr - y * wi, x * wi + y * wr

    def outer(c, read):
        d = jnp.concatenate([read(h) for h in range(2)], axis=1).astype(BF)
        x = mm(first[...], jnp.concatenate([d, d], axis=0))
        ar, ai = rotate(x[:n, :half], x[n:, :half], wre[:, :half], wim[:, :half])
        br, bi = rotate(x[:n, half:], x[n:, half:], wre[:, half:], wim[:, half:])
        odd_r, odd_i = rotate(ar - br, ai - bi, ure[...], uim[...])
        rows = slice(c * n, (c + 1) * n)
        for i, value in enumerate((ar + br, ai + bi, odd_r, odd_i)):
            lanes = slice(i * half, (i + 1) * half)
            z_hi[rows, lanes], z_lo[rows, lanes] = split(value)

    def inner(rows, lanes, high_table, low_table):
        high, low = z_hi[rows, lanes], z_lo[rows, lanes]
        return mm(high, high_table[...]) + mm(low, high_table[...]) + mm(high, low_table[...])

    def group_rows(g):
        return slice(g * GROUP * n, (g + 1) * GROUP * n)

    both = [slice(par * tok, (par + 1) * tok) for par in range(2)]

    def keep(g):
        for lanes in both:
            spec[group_rows(g), lanes] = inner(group_rows(g), lanes, fwd_hi, fwd_lo)

    def multiply(g):
        for lanes in both:
            x, hx = inner(group_rows(g), lanes, fwd_hi, fwd_lo), spec[group_rows(g), lanes]
            pr, pi = rotate(x[:, :half], x[:, half:], hx[:, :half], hx[:, half:])
            z_hi[group_rows(g), lanes], z_lo[group_rows(g), lanes] = split(
                jnp.concatenate([pr, pi], axis=1)
            )

    def back(g):
        even = inner(group_rows(g), both[0], inv_hi, inv_lo)
        odd = inner(group_rows(g), both[1], inv_hi, inv_lo)
        tr, ti = rotate(odd[:, :half], odd[:, half:], ure[...], -uim[...])
        odd = jnp.concatenate([tr, ti], axis=1)
        waves[0, group_rows(g)] = even + odd
        waves[1, group_rows(g)] = even - odd

    def close_up(g, h):
        lanes = slice(h * half, (h + 1) * half)
        for c in range(g * GROUP, (g + 1) * GROUP, 2):
            sides = []
            for cc in (c, c + 1):
                u = waves[h, cc * n:(cc + 1) * n]
                vr, vi = rotate(u[:, :half], u[:, half:], wre[:, lanes], -wim[:, lanes])
                sides.append(jnp.concatenate([vr, vi], axis=0))
            v_hi, v_lo = split(jnp.concatenate(sides, axis=1))
            y = mm(last[...], jnp.concatenate([v_hi, v_hi, v_lo], axis=0))
            conv_f[h, pl.ds(c, n, stride=chans), :] = y[:, :half]
            conv_f[h, pl.ds(c + 1, n, stride=chans), :] = y[:, half:]

    groups = chans // GROUP
    landed(recv_f, fwd_recv.at[0])
    for h in range(2):
        stage[h] = recv_f[:, h].reshape(n * chans, half).astype(F32)
    for g in range(groups):
        for c in range(g * GROUP, (g + 1) * GROUP):
            outer(c, lambda h: stage[h, pl.ds(c, n, stride=chans), :])
    for g in range(groups):
        keep(g)

    for q in range(CHUNKS):
        landed(recv_p.at[q], fwd_recv.at[1 + q])
        stage[q] = recv_p[q].reshape(n * 2 * some, half).astype(F32)
        mine_now = range(q * groups // CHUNKS, (q + 1) * groups // CHUNKS)
        for g in mine_now:
            for c in range(g * GROUP, (g + 1) * GROUP):
                outer(c, lambda h: stage[
                    q, pl.ds(h * some + c - q * some, n, stride=2 * some), :
                ])
        for g in mine_now:
            multiply(g)
        for g in mine_now:
            back(g)
        for h in range(2):
            for g in mine_now:
                close_up(g, h)
            if q == CHUNKS - 1:
                ret_s[h] = conv_f[h].astype(BF).reshape(n, chans, half)
                spread(ret_s.at[h], ret_r.at[h], ret_send.at[h], ret_recv.at[h])

    for i in range(13, 16):
        loads[i].wait()

    part = cols // PARTS

    def pair(slot, h, src, dst, target):
        return pltpu.make_async_remote_copy(
            src_ref=src,
            dst_ref=dst,
            send_sem=pair_send.at[slot, h],
            recv_sem=pair_recv.at[slot, h],
            device_id={"fsdp": target},
            device_id_type=MESH,
        )

    def partial(h, owner, piece):
        start = pl.multiple_of(owner * cols + piece * part, part)
        return mm(gated[h], weight[:, pl.ds(start, part)])

    def to_sib(h, piece):
        return pair(piece, h, sib_s.at[h, piece], sib_r.at[h, piece], sibling)

    def to_cross(h, piece):
        return pair(PARTS + piece, h, cross_s.at[h, piece], cross_r.at[h, piece], across)

    def own_sib(h, piece):
        return pair(2 * PARTS + piece, h, own_s.at[h, piece], own_r.at[h, piece], sibling)

    def gate(h):
        rows = slice(h * half, (h + 1) * half)
        for j in range(width // block):
            lanes = slice(j * block, (j + 1) * block)
            conv = ret_r[h, j * peers:(j + 1) * peers].reshape(block, half).astype(F32).T
            product = keys[rows, lanes].astype(F32) * vals[rows, lanes].astype(F32)
            mixed = conv + skip[:, lanes] * product
            gated[h, :, lanes] = (quer[rows, lanes].astype(F32) * mixed).astype(BF)

    def leave(h):
        for piece in range(PARTS):
            sib_s[h, piece] = partial(h, beyond, piece).astype(BF)
            to_sib(h, piece).start()
        for piece in range(PARTS):
            near = partial(h, across, piece)
            to_sib(h, piece).wait_recv()
            cross_s[h, piece] = (near + sib_r[h, piece].astype(F32)).astype(BF)
            to_cross(h, piece).start()

    def stay(h):
        for piece in range(PARTS):
            own_s[h, piece] = partial(h, sibling, piece).astype(BF)
            own_sib(h, piece).start()
        for piece in range(PARTS):
            mine[h, piece] = partial(h, col, piece)

    def finish(h):
        rows = slice(h * half, (h + 1) * half)
        for piece in range(PARTS):
            own_sib(h, piece).wait_recv()
            to_cross(h, piece).wait_recv()
            out_ref[rows, piece * part:(piece + 1) * part] = (
                mine[h, piece] + own_r[h, piece].astype(F32) + cross_r[h, piece].astype(F32)
            ).astype(BF)

    landed(ret_r.at[0], ret_recv.at[0])
    gate(0)
    leave(0)
    stay(0)
    landed(ret_r.at[1], ret_recv.at[1])
    gate(1)
    leave(1)
    stay(1)
    finish(0)
    finish(1)
    for h in range(2):
        for piece in range(PARTS):
            to_sib(h, piece).wait_send()
            to_cross(h, piece).wait_send()
            own_sib(h, piece).wait_send()
    landed(send_f, fwd_send.at[0])
    for q in range(CHUNKS):
        landed(send_p.at[q], fwd_send.at[1 + q])
    landed(ret_s.at[0], ret_send.at[0])
    landed(ret_s.at[1], ret_send.at[1])


def body(queries, keys, values, filters, skip_weight, out_weight):
    n = lax.axis_size("seq")
    tok, width = keys.shape
    cols = width
    half = tok // 2
    chans = width // n
    tables = [jnp.asarray(t) for t in make_tables(n, tok)]
    operands = (
        filters, keys, values, *tables, queries, skip_weight.reshape(1, width), out_weight,
    )
    dma = pltpu.SemaphoreType.DMA
    scratch = [pltpu.VMEM(x.shape, x.dtype) for x in operands] + [
        pltpu.VMEM((n, 2, chans, half), BF),
        pltpu.VMEM((CHUNKS, n, 2 * chans // CHUNKS, half), BF),
        pltpu.VMEM((n, 2, chans, half), BF),
        pltpu.VMEM((CHUNKS, n, 2 * chans // CHUNKS, half), BF),
        pltpu.VMEM((2, n, chans, half), BF),
        pltpu.VMEM((2, n, chans, half), BF),
        pltpu.VMEM((2, n * chans, half), F32),
        pltpu.VMEM((2, n * chans, half), F32),
        pltpu.VMEM((n * chans, 2 * tok), BF),
        pltpu.VMEM((n * chans, 2 * tok), BF),
        pltpu.VMEM((2, n * chans, tok), F32),
        pltpu.VMEM((n * chans, 2 * tok), F32),
        pltpu.VMEM((2, half, width), BF),
        pltpu.VMEM((2, PARTS, half, cols // PARTS), F32),
        pltpu.VMEM((2, PARTS, half, cols // PARTS), BF),
        pltpu.VMEM((2, PARTS, half, cols // PARTS), BF),
        pltpu.VMEM((2, PARTS, half, cols // PARTS), BF),
        pltpu.VMEM((2, PARTS, half, cols // PARTS), BF),
        pltpu.VMEM((2, PARTS, half, cols // PARTS), BF),
        pltpu.VMEM((2, PARTS, half, cols // PARTS), BF),
        dma((16,)),
        dma((1 + CHUNKS,)),
        dma((1 + CHUNKS,)),
        dma((2,)),
        dma((2,)),
        dma((3 * PARTS, 2)),
        dma((3 * PARTS, 2)),
    ]
    flops = 2 * chans * n * 3 * (2 * tok) * tok * 3 + 2 * tok * width * 4 * cols
    return pl.pallas_call(
        kernel,
        out_shape=jax.ShapeDtypeStruct((tok, cols), BF),
        in_specs=[pl.BlockSpec(memory_space=pl.ANY)] * len(operands),
        out_specs=pl.BlockSpec(memory_space=pltpu.VMEM),
        scratch_shapes=scratch,
        compiler_params=pltpu.CompilerParams(
            collective_id=0, has_side_effects=True, vmem_limit_bytes=62 * 1024 * 1024
        ),
        cost_estimate=pl.CostEstimate(
            flops=flops, bytes_accessed=16 * 1024 * 1024, transcendentals=0
        ),
        name="hyena",
    )(*operands)


def solution(mesh):
    in_specs = (
        P("seq", "fsdp"),
        P("seq", "fsdp"),
        P("seq", "fsdp"),
        P("seq", "fsdp"),
        P("fsdp"),
        P("fsdp", None),
    )
    out_specs = P("seq", "fsdp")
    return jax.shard_map(body, mesh=mesh, in_specs=in_specs, out_specs=out_specs, check_vma=False)
```

```python
import functools
import math

import jax
import jax.numpy as jnp
import ml_dtypes
import numpy as np
from jax import lax
from jax.experimental import pallas as pl
from jax.experimental.pallas import tpu as pltpu
from jax.sharding import PartitionSpec as P

MESH = pl.DeviceIdType.MESH
BF = jnp.bfloat16
F32 = jnp.float32
GROUP = 4
PARTS = 4
FIRST = 2
CHUNKS = 2
ORDER = (4, 3, 5, 2, 6, 1, 7, 0)


def split_np(table):
    high = table.astype(np.float32).astype(ml_dtypes.bfloat16)
    low = (table - high.astype(np.float64)).astype(np.float32).astype(ml_dtypes.bfloat16)
    return high, low


def make_tables(n_blocks, width):
    half = width // 2
    total = n_blocks * width
    theta = np.arange(n_blocks) + 0.25
    lanes = np.arange(half)
    outer = 2 * math.pi * np.outer(theta, np.arange(n_blocks)) / n_blocks
    twist = 2 * math.pi * np.outer(theta, np.arange(width)) / total
    inner = 2 * math.pi * (np.outer(lanes, lanes) % half) / half
    cos, sin = np.cos(inner), np.sin(inner)
    turn = 2 * math.pi * lanes[None, :] / width
    first = np.concatenate([np.cos(outer), -np.sin(outer)], axis=0)
    last = np.concatenate([np.cos(outer).T, -np.sin(outer).T], axis=1) / total
    first_hi, first_lo = split_np(first)
    last_hi, last_lo = split_np(last)
    return (
        np.concatenate([first_hi, first_lo], axis=1),
        np.cos(twist).astype(np.float32),
        (-np.sin(twist)).astype(np.float32),
        np.cos(turn).astype(np.float32),
        (-np.sin(turn)).astype(np.float32),
        *split_np(np.block([[cos, -sin], [sin, cos]])),
        *split_np(np.block([[cos, sin], [-sin, cos]])),
        np.concatenate([last_hi, last_lo, last_hi], axis=1),
    )


def split(x):
    high = x.astype(BF)
    return high, (x - high.astype(F32)).astype(BF)


def mm(a, b):
    return jnp.dot(a, b, preferred_element_type=F32)


def kernel(*refs):
    hbm = refs[:16]
    out_ref = refs[16]
    vm = refs[17:33]
    (send_f, send_p, recv_f, recv_p, ret_s, ret_r, stage, conv_f, z_hi, z_lo, waves, spec,
     gated, mine, sib_s, sib_r, own_s, own_r, cross_s, cross_r,
     local_sem, fwd_send, fwd_recv, ret_send, ret_recv, pair_send, pair_recv) = refs[33:]
    (filt, keys, vals, first, wre, wim, ure, uim, fwd_hi, fwd_lo, inv_hi, inv_lo, last,
     quer, skip, weight) = vm

    me = lax.axis_index("seq")
    col = lax.axis_index("fsdp")
    n = send_f.shape[0]
    chans = send_f.shape[2]
    tok = keys.shape[0]
    half = tok // 2
    width = keys.shape[1]
    cols = out_ref.shape[1]
    some = chans // CHUNKS
    block = min(128, width)
    peers = block // chans
    sibling = col + 1 - 2 * (col % 2)
    across = (col + 2) % 4
    beyond = (sibling + 2) % 4

    loads = [pltpu.make_async_copy(hbm[i], vm[i], local_sem.at[i]) for i in range(16)]
    for copy in loads[:3]:
        copy.start()

    barrier = pltpu.get_barrier_semaphore()

    def greet(i, carry):
        pl.semaphore_signal(
            barrier, inc=1, device_id={"seq": (me + i) % n}, device_id_type=MESH
        )
        return carry

    for other in (sibling, across):
        pl.semaphore_signal(barrier, inc=1, device_id={"fsdp": other}, device_id_type=MESH)
    lax.fori_loop(1, n, greet, 0)

    def spread(src, dst, send_sem, recv_sem):
        def go(i, carry):
            peer = (me + i) % n
            pltpu.make_async_remote_copy(
                src_ref=src.at[peer],
                dst_ref=dst.at[me],
                send_sem=send_sem,
                recv_sem=recv_sem,
                device_id={"seq": peer},
                device_id_type=MESH,
            ).start()
            return carry

        run = min(8, n)
        for at in ORDER if n == 64 else range(n // run):
            lax.fori_loop(max(1, at * run), (at + 1) * run, go, 0)
        dst[me] = src[me]

    def landed(buf, sem):
        part = buf.at[pl.ds(0, n - 1)]
        pltpu.make_async_copy(part, part, sem).wait()

    loads[0].wait()
    for h in range(2):
        for j in range(width // block):
            x = filt[h * half:(h + 1) * half, j * block:(j + 1) * block]
            send_f[j * peers:(j + 1) * peers, h] = x.T.astype(BF).reshape(peers, chans, half)
    pl.semaphore_wait(barrier, n + 1)
    spread(send_f, recv_f, fwd_send.at[0], fwd_recv.at[0])
    for copy in loads[3:13]:
        copy.start()
    loads[1].wait()
    loads[2].wait()
    for j in range(width // block):
        lanes = slice(j * block, (j + 1) * block)
        turned = []
        for h in range(2):
            rows = slice(h * half, (h + 1) * half)
            x = keys[rows, lanes].astype(F32) * vals[rows, lanes].astype(F32)
            turned.append(x.T.reshape(peers, chans, half))
        for q in range(CHUNKS):
            sub = slice(q * some, (q + 1) * some)
            send_p[q, j * peers:(j + 1) * peers] = jnp.concatenate(
                [x[:, sub] for x in turned], axis=1
            ).astype(BF)
    for q in range(CHUNKS):
        spread(send_p.at[q], recv_p.at[q], fwd_send.at[1 + q], fwd_recv.at[1 + q])
    for copy in loads[13:]:
        copy.start()
    for i in range(3, 13):
        loads[i].wait()

    def rotate(x, y, wr, wi):
        return x * wr - y * wi, x * wi + y * wr

    def outer(c, read):
        d = jnp.concatenate([read(h) for h in range(2)], axis=1).astype(BF)
        x = mm(first[...], jnp.concatenate([d, d], axis=0))
        ar, ai = rotate(x[:n, :half], x[n:, :half], wre[:, :half], wim[:, :half])
        br, bi = rotate(x[:n, half:], x[n:, half:], wre[:, half:], wim[:, half:])
        odd_r, odd_i = rotate(ar - br, ai - bi, ure[...], uim[...])
        rows = slice(c * n, (c + 1) * n)
        for i, value in enumerate((ar + br, ai + bi, odd_r, odd_i)):
            lanes = slice(i * half, (i + 1) * half)
            z_hi[rows, lanes], z_lo[rows, lanes] = split(value)

    def inner(rows, lanes, high_table, low_table):
        high, low = z_hi[rows, lanes], z_lo[rows, lanes]
        return mm(high, high_table[...]) + mm(low, high_table[...]) + mm(high, low_table[...])

    def group_rows(g):
        return slice(g * GROUP * n, (g + 1) * GROUP * n)

    both = [slice(par * tok, (par + 1) * tok) for par in range(2)]

    def keep(g):
        for lanes in both:
            spec[group_rows(g), lanes] = inner(group_rows(g), lanes, fwd_hi, fwd_lo)

    def multiply(g):
        for lanes in both:
            x, hx = inner(group_rows(g), lanes, fwd_hi, fwd_lo), spec[group_rows(g), lanes]
            pr, pi = rotate(x[:, :half], x[:, half:], hx[:, :half], hx[:, half:])
            z_hi[group_rows(g), lanes], z_lo[group_rows(g), lanes] = split(
                jnp.concatenate([pr, pi], axis=1)
            )

    def back(g):
        even = inner(group_rows(g), both[0], inv_hi, inv_lo)
        odd = inner(group_rows(g), both[1], inv_hi, inv_lo)
        tr, ti = rotate(odd[:, :half], odd[:, half:], ure[...], -uim[...])
        odd = jnp.concatenate([tr, ti], axis=1)
        waves[0, group_rows(g)] = even + odd
        waves[1, group_rows(g)] = even - odd

    def close_up(g, h):
        lanes = slice(h * half, (h + 1) * half)
        for c in range(g * GROUP, (g + 1) * GROUP, 2):
            sides = []
            for cc in (c, c + 1):
                u = waves[h, cc * n:(cc + 1) * n]
                vr, vi = rotate(u[:, :half], u[:, half:], wre[:, lanes], -wim[:, lanes])
                sides.append(jnp.concatenate([vr, vi], axis=0))
            v_hi, v_lo = split(jnp.concatenate(sides, axis=1))
            y = mm(last[...], jnp.concatenate([v_hi, v_hi, v_lo], axis=0))
            conv_f[h, pl.ds(c, n, stride=chans), :] = y[:, :half]
            conv_f[h, pl.ds(c + 1, n, stride=chans), :] = y[:, half:]

    groups = chans // GROUP
    landed(recv_f, fwd_recv.at[0])
    for h in range(2):
        stage[h] = recv_f[:, h].reshape(n * chans, half).astype(F32)
    for g in range(groups):
        for c in range(g * GROUP, (g + 1) * GROUP):
            outer(c, lambda h: stage[h, pl.ds(c, n, stride=chans), :])
    for g in range(groups):
        keep(g)

    for q in range(CHUNKS):
        landed(recv_p.at[q], fwd_recv.at[1 + q])
        stage[q] = recv_p[q].reshape(n * 2 * some, half).astype(F32)
        mine_now = range(q * groups // CHUNKS, (q + 1) * groups // CHUNKS)
        for g in mine_now:
            for c in range(g * GROUP, (g + 1) * GROUP):
                outer(c, lambda h: stage[
                    q, pl.ds(h * some + c - q * some, n, stride=2 * some), :
                ])
        for g in mine_now:
            multiply(g)
        for g in mine_now:
            back(g)
        for h in range(2):
            for g in mine_now:
                close_up(g, h)
            if q == CHUNKS - 1:
                ret_s[h] = conv_f[h].astype(BF).reshape(n, chans, half)
                spread(ret_s.at[h], ret_r.at[h], ret_send.at[h], ret_recv.at[h])

    for i in range(13, 16):
        loads[i].wait()

    part = cols // PARTS

    def pair(slot, src, dst, target):
        return pltpu.make_async_remote_copy(
            src_ref=src,
            dst_ref=dst,
            send_sem=pair_send.at[slot],
            recv_sem=pair_recv.at[slot],
            device_id={"fsdp": target},
            device_id_type=MESH,
        )

    def partial(rows, owner, piece):
        start = pl.multiple_of(owner * cols + piece * part, part)
        return mm(gated[rows], weight[:, pl.ds(start, part)])

    def token_rows(h):
        return slice(h * half, (h + 1) * half)

    def to_sib(h, p):
        return pair(h * PARTS + p, sib_s.at[h, p], sib_r.at[h, p], sibling)

    def to_cross(h, p):
        return pair((2 + h) * PARTS + p, cross_s.at[h, p], cross_r.at[h, p], across)

    def own_sib(p):
        return pair(4 * PARTS + p, own_s.at[p], own_r.at[p], sibling)

    def gate(h):
        rows = token_rows(h)
        for j in range(width // block):
            lanes = slice(j * block, (j + 1) * block)
            conv = ret_r[h, j * peers:(j + 1) * peers].reshape(block, half).astype(F32).T
            product = keys[rows, lanes].astype(F32) * vals[rows, lanes].astype(F32)
            mixed = conv + skip[:, lanes] * product
            gated[rows, lanes] = (quer[rows, lanes].astype(F32) * mixed).astype(BF)

    def far(h, p):
        sib_s[h, p] = partial(token_rows(h), beyond, p).astype(BF)
        to_sib(h, p).start()

    def near(h, p):
        own = partial(token_rows(h), across, p)
        to_sib(h, p).wait_recv()
        cross_s[h, p] = (own + sib_r[h, p].astype(F32)).astype(BF)
        to_cross(h, p).start()

    landed(ret_r.at[0], ret_recv.at[0])
    gate(0)
    for p in range(PARTS):
        far(0, p)
    for p in range(FIRST):
        near(0, p)
    landed(ret_r.at[1], ret_recv.at[1])
    gate(1)
    for p in range(PARTS):
        far(1, p)
    for p in range(FIRST, PARTS):
        near(0, p)
    for p in range(PARTS):
        near(1, p)
    everything = slice(0, tok)
    for p in range(PARTS):
        own_s[p] = partial(everything, sibling, p).astype(BF)
        own_sib(p).start()
    for p in range(PARTS):
        mine[p] = partial(everything, col, p)
    for p in range(PARTS):
        own_sib(p).wait_recv()
        mine[p] += own_r[p].astype(F32)
    for h in range(2):
        for p in range(PARTS):
            to_cross(h, p).wait_recv()
            out_ref[token_rows(h), p * part:(p + 1) * part] = (
                mine[p, token_rows(h)] + cross_r[h, p].astype(F32)
            ).astype(BF)
    for p in range(PARTS):
        own_sib(p).wait_send()
        for h in range(2):
            to_sib(h, p).wait_send()
            to_cross(h, p).wait_send()

    landed(send_f, fwd_send.at[0])
    for q in range(CHUNKS):
        landed(send_p.at[q], fwd_send.at[1 + q])
    landed(ret_s.at[0], ret_send.at[0])
    landed(ret_s.at[1], ret_send.at[1])


def body(queries, keys, values, filters, skip_weight, out_weight):
    n = lax.axis_size("seq")
    tok, width = keys.shape
    cols = width
    half = tok // 2
    chans = width // n
    tables = [jnp.asarray(t) for t in make_tables(n, tok)]
    operands = (
        filters, keys, values, *tables, queries, skip_weight.reshape(1, width), out_weight,
    )
    dma = pltpu.SemaphoreType.DMA
    scratch = [pltpu.VMEM(x.shape, x.dtype) for x in operands] + [
        pltpu.VMEM((n, 2, chans, half), BF),
        pltpu.VMEM((CHUNKS, n, 2 * chans // CHUNKS, half), BF),
        pltpu.VMEM((n, 2, chans, half), BF),
        pltpu.VMEM((CHUNKS, n, 2 * chans // CHUNKS, half), BF),
        pltpu.VMEM((2, n, chans, half), BF),
        pltpu.VMEM((2, n, chans, half), BF),
        pltpu.VMEM((2, n * chans, half), F32),
        pltpu.VMEM((2, n * chans, half), F32),
        pltpu.VMEM((n * chans, 2 * tok), BF),
        pltpu.VMEM((n * chans, 2 * tok), BF),
        pltpu.VMEM((2, n * chans, tok), F32),
        pltpu.VMEM((n * chans, 2 * tok), F32),
        pltpu.VMEM((tok, width), BF),
        pltpu.VMEM((PARTS, tok, cols // PARTS), F32),
        pltpu.VMEM((2, PARTS, half, cols // PARTS), BF),
        pltpu.VMEM((2, PARTS, half, cols // PARTS), BF),
        pltpu.VMEM((PARTS, tok, cols // PARTS), BF),
        pltpu.VMEM((PARTS, tok, cols // PARTS), BF),
        pltpu.VMEM((2, PARTS, half, cols // PARTS), BF),
        pltpu.VMEM((2, PARTS, half, cols // PARTS), BF),
        dma((16,)),
        dma((1 + CHUNKS,)),
        dma((1 + CHUNKS,)),
        dma((2,)),
        dma((2,)),
        dma((5 * PARTS,)),
        dma((5 * PARTS,)),
    ]
    flops = 2 * chans * n * 3 * (2 * tok) * tok * 3 + 2 * tok * width * 4 * cols
    return pl.pallas_call(
        kernel,
        out_shape=jax.ShapeDtypeStruct((tok, cols), BF),
        in_specs=[pl.BlockSpec(memory_space=pl.ANY)] * len(operands),
        out_specs=pl.BlockSpec(memory_space=pltpu.VMEM),
        scratch_shapes=scratch,
        compiler_params=pltpu.CompilerParams(
            collective_id=0, has_side_effects=True, vmem_limit_bytes=62 * 1024 * 1024
        ),
        cost_estimate=pl.CostEstimate(
            flops=flops, bytes_accessed=16 * 1024 * 1024, transcendentals=0
        ),
        name="hyena",
    )(*operands)


def solution(mesh):
    in_specs = (
        P("seq", "fsdp"),
        P("seq", "fsdp"),
        P("seq", "fsdp"),
        P("seq", "fsdp"),
        P("fsdp"),
        P("fsdp", None),
    )
    out_specs = P("seq", "fsdp")
    return jax.shard_map(body, mesh=mesh, in_specs=in_specs, out_specs=out_specs, check_vma=False)
```

```python
import functools
import math

import jax
import jax.numpy as jnp
import ml_dtypes
import numpy as np
from jax import lax
from jax.experimental import pallas as pl
from jax.experimental.pallas import tpu as pltpu
from jax.sharding import PartitionSpec as P

MESH = pl.DeviceIdType.MESH
BF = jnp.bfloat16
F32 = jnp.float32
GROUP = 4
PARTS = 2
FIRST = 1
CHUNKS = 2
ORDER = (4, 3, 5, 2, 6, 1, 7, 0)


def split_np(table):
    high = table.astype(np.float32).astype(ml_dtypes.bfloat16)
    low = (table - high.astype(np.float64)).astype(np.float32).astype(ml_dtypes.bfloat16)
    return high, low


def make_tables(n_blocks, width):
    half = width // 2
    total = n_blocks * width
    theta = np.arange(n_blocks) + 0.25
    lanes = np.arange(half)
    outer = 2 * math.pi * np.outer(theta, np.arange(n_blocks)) / n_blocks
    twist = 2 * math.pi * np.outer(theta, np.arange(width)) / total
    inner = 2 * math.pi * (np.outer(lanes, lanes) % half) / half
    cos, sin = np.cos(inner), np.sin(inner)
    turn = 2 * math.pi * lanes[None, :] / width
    first = np.concatenate([np.cos(outer), -np.sin(outer)], axis=0)
    last = np.concatenate([np.cos(outer).T, -np.sin(outer).T], axis=1) / total
    first_hi, first_lo = split_np(first)
    last_hi, last_lo = split_np(last)
    return (
        np.concatenate([first_hi, first_lo], axis=1),
        np.cos(twist).astype(np.float32),
        (-np.sin(twist)).astype(np.float32),
        np.cos(turn).astype(np.float32),
        (-np.sin(turn)).astype(np.float32),
        *split_np(np.block([[cos, -sin], [sin, cos]])),
        *split_np(np.block([[cos, sin], [-sin, cos]])),
        np.concatenate([last_hi, last_lo, last_hi], axis=1),
    )


def split(x):
    high = x.astype(BF)
    return high, (x - high.astype(F32)).astype(BF)


def mm(a, b):
    return jnp.dot(a, b, preferred_element_type=F32)


def kernel(*refs):
    hbm = refs[:16]
    out_ref = refs[16]
    vm = refs[17:33]
    (send_f, send_p, recv_f, recv_p, ret_s, ret_r, stage, conv_f, z_hi, z_lo, waves, spec,
     gated, mine, sib_s, sib_r, own_s, own_r, cross_s, cross_r,
     local_sem, fwd_send, fwd_recv, ret_send, ret_recv, pair_send, pair_recv) = refs[33:]
    (filt, keys, vals, first, wre, wim, ure, uim, fwd_hi, fwd_lo, inv_hi, inv_lo, last,
     quer, skip, weight) = vm

    me = lax.axis_index("seq")
    col = lax.axis_index("fsdp")
    n = send_f.shape[0]
    chans = send_f.shape[2]
    tok = keys.shape[0]
    half = tok // 2
    width = keys.shape[1]
    cols = out_ref.shape[1]
    some = chans // CHUNKS
    block = min(128, width)
    peers = block // chans
    sibling = col + 1 - 2 * (col % 2)
    across = (col + 2) % 4
    beyond = (sibling + 2) % 4

    loads = [pltpu.make_async_copy(hbm[i], vm[i], local_sem.at[i]) for i in range(16)]
    for copy in loads[:3]:
        copy.start()

    barrier = pltpu.get_barrier_semaphore()

    def greet(i, carry):
        pl.semaphore_signal(
            barrier, inc=1, device_id={"seq": (me + i) % n}, device_id_type=MESH
        )
        return carry

    for other in (sibling, across):
        pl.semaphore_signal(barrier, inc=1, device_id={"fsdp": other}, device_id_type=MESH)
    lax.fori_loop(1, n, greet, 0)

    def spread(src, dst, send_sem, recv_sem):
        def go(i, carry):
            peer = (me + i) % n
            pltpu.make_async_remote_copy(
                src_ref=src.at[peer],
                dst_ref=dst.at[me],
                send_sem=send_sem,
                recv_sem=recv_sem,
                device_id={"seq": peer},
                device_id_type=MESH,
            ).start()
            return carry

        run = min(8, n)
        for at in ORDER if n == 64 else range(n // run):
            lax.fori_loop(max(1, at * run), (at + 1) * run, go, 0)
        dst[me] = src[me]

    def landed(buf, sem):
        part = buf.at[pl.ds(0, n - 1)]
        pltpu.make_async_copy(part, part, sem).wait()

    loads[0].wait()
    for h in range(2):
        for j in range(width // block):
            x = filt[h * half:(h + 1) * half, j * block:(j + 1) * block]
            send_f[j * peers:(j + 1) * peers, h] = x.T.astype(BF).reshape(peers, chans, half)
    pl.semaphore_wait(barrier, n + 1)
    spread(send_f, recv_f, fwd_send.at[0], fwd_recv.at[0])
    for copy in loads[3:13]:
        copy.start()
    loads[1].wait()
    loads[2].wait()
    for j in range(width // block):
        lanes = slice(j * block, (j + 1) * block)
        turned = []
        for h in range(2):
            rows = slice(h * half, (h + 1) * half)
            x = keys[rows, lanes].astype(F32) * vals[rows, lanes].astype(F32)
            turned.append(x.T.reshape(peers, chans, half))
        for q in range(CHUNKS):
            sub = slice(q * some, (q + 1) * some)
            send_p[q, j * peers:(j + 1) * peers] = jnp.concatenate(
                [x[:, sub] for x in turned], axis=1
            ).astype(BF)
    for q in range(CHUNKS):
        spread(send_p.at[q], recv_p.at[q], fwd_send.at[1 + q], fwd_recv.at[1 + q])
    for copy in loads[13:]:
        copy.start()
    for i in range(3, 13):
        loads[i].wait()

    def rotate(x, y, wr, wi):
        return x * wr - y * wi, x * wi + y * wr

    def outer(c, read):
        d = jnp.concatenate([read(h) for h in range(2)], axis=1).astype(BF)
        x = mm(first[...], jnp.concatenate([d, d], axis=0))
        ar, ai = rotate(x[:n, :half], x[n:, :half], wre[:, :half], wim[:, :half])
        br, bi = rotate(x[:n, half:], x[n:, half:], wre[:, half:], wim[:, half:])
        odd_r, odd_i = rotate(ar - br, ai - bi, ure[...], uim[...])
        rows = slice(c * n, (c + 1) * n)
        for i, value in enumerate((ar + br, ai + bi, odd_r, odd_i)):
            lanes = slice(i * half, (i + 1) * half)
            z_hi[rows, lanes], z_lo[rows, lanes] = split(value)

    def inner(rows, lanes, high_table, low_table):
        high, low = z_hi[rows, lanes], z_lo[rows, lanes]
        return mm(high, high_table[...]) + mm(low, high_table[...]) + mm(high, low_table[...])

    def group_rows(g):
        return slice(g * GROUP * n, (g + 1) * GROUP * n)

    both = [slice(par * tok, (par + 1) * tok) for par in range(2)]

    def keep(g):
        for lanes in both:
            spec[group_rows(g), lanes] = inner(group_rows(g), lanes, fwd_hi, fwd_lo)

    def multiply(g):
        for lanes in both:
            x, hx = inner(group_rows(g), lanes, fwd_hi, fwd_lo), spec[group_rows(g), lanes]
            pr, pi = rotate(x[:, :half], x[:, half:], hx[:, :half], hx[:, half:])
            z_hi[group_rows(g), lanes], z_lo[group_rows(g), lanes] = split(
                jnp.concatenate([pr, pi], axis=1)
            )

    def back(g):
        even = inner(group_rows(g), both[0], inv_hi, inv_lo)
        odd = inner(group_rows(g), both[1], inv_hi, inv_lo)
        tr, ti = rotate(odd[:, :half], odd[:, half:], ure[...], -uim[...])
        odd = jnp.concatenate([tr, ti], axis=1)
        waves[0, group_rows(g)] = even + odd
        waves[1, group_rows(g)] = even - odd

    def close_up(g, h):
        lanes = slice(h * half, (h + 1) * half)
        for c in range(g * GROUP, (g + 1) * GROUP, 2):
            sides = []
            for cc in (c, c + 1):
                u = waves[h, cc * n:(cc + 1) * n]
                vr, vi = rotate(u[:, :half], u[:, half:], wre[:, lanes], -wim[:, lanes])
                sides.append(jnp.concatenate([vr, vi], axis=0))
            v_hi, v_lo = split(jnp.concatenate(sides, axis=1))
            y = mm(last[...], jnp.concatenate([v_hi, v_hi, v_lo], axis=0))
            conv_f[h, pl.ds(c, n, stride=chans), :] = y[:, :half]
            conv_f[h, pl.ds(c + 1, n, stride=chans), :] = y[:, half:]

    groups = chans // GROUP
    landed(recv_f, fwd_recv.at[0])
    for h in range(2):
        stage[h] = recv_f[:, h].reshape(n * chans, half).astype(F32)
    for g in range(groups):
        for c in range(g * GROUP, (g + 1) * GROUP):
            outer(c, lambda h: stage[h, pl.ds(c, n, stride=chans), :])
    for g in range(groups):
        keep(g)

    for q in range(CHUNKS):
        landed(recv_p.at[q], fwd_recv.at[1 + q])
        stage[q] = recv_p[q].reshape(n * 2 * some, half).astype(F32)
        mine_now = range(q * groups // CHUNKS, (q + 1) * groups // CHUNKS)
        for g in mine_now:
            for c in range(g * GROUP, (g + 1) * GROUP):
                outer(c, lambda h: stage[
                    q, pl.ds(h * some + c - q * some, n, stride=2 * some), :
                ])
        for g in mine_now:
            multiply(g)
        for g in mine_now:
            back(g)
        for h in range(2):
            for g in mine_now:
                close_up(g, h)
            if q == CHUNKS - 1:
                ret_s[h] = conv_f[h].astype(BF).reshape(n, chans, half)
                spread(ret_s.at[h], ret_r.at[h], ret_send.at[h], ret_recv.at[h])

    for i in range(13, 16):
        loads[i].wait()

    part = cols // PARTS

    def pair(slot, src, dst, target):
        return pltpu.make_async_remote_copy(
            src_ref=src,
            dst_ref=dst,
            send_sem=pair_send.at[slot],
            recv_sem=pair_recv.at[slot],
            device_id={"fsdp": target},
            device_id_type=MESH,
        )

    def partial(rows, owner, piece):
        start = pl.multiple_of(owner * cols + piece * part, part)
        return mm(gated[rows], weight[:, pl.ds(start, part)])

    def token_rows(h):
        return slice(h * half, (h + 1) * half)

    def to_sib(h, p):
        return pair(h * PARTS + p, sib_s.at[h, p], sib_r.at[h, p], sibling)

    def to_cross(h, p):
        return pair((2 + h) * PARTS + p, cross_s.at[h, p], cross_r.at[h, p], across)

    def own_sib(p):
        return pair(4 * PARTS + p, own_s.at[p], own_r.at[p], sibling)

    def gate(h):
        rows = token_rows(h)
        for j in range(width // block):
            lanes = slice(j * block, (j + 1) * block)
            conv = ret_r[h, j * peers:(j + 1) * peers].reshape(block, half).astype(F32).T
            product = keys[rows, lanes].astype(F32) * vals[rows, lanes].astype(F32)
            mixed = conv + skip[:, lanes] * product
            gated[rows, lanes] = (quer[rows, lanes].astype(F32) * mixed).astype(BF)

    def far(h, p):
        sib_s[h, p] = partial(token_rows(h), beyond, p).astype(BF)
        to_sib(h, p).start()

    def near(h, p):
        own = partial(token_rows(h), across, p)
        to_sib(h, p).wait_recv()
        cross_s[h, p] = (own + sib_r[h, p].astype(F32)).astype(BF)
        to_cross(h, p).start()

    landed(ret_r.at[0], ret_recv.at[0])
    gate(0)
    for p in range(PARTS):
        far(0, p)
    for p in range(FIRST):
        near(0, p)
    landed(ret_r.at[1], ret_recv.at[1])
    gate(1)
    for p in range(PARTS):
        far(1, p)
    for p in range(FIRST, PARTS):
        near(0, p)
    for p in range(PARTS):
        near(1, p)
    everything = slice(0, tok)
    for p in range(PARTS):
        own_s[p] = partial(everything, sibling, p).astype(BF)
        own_sib(p).start()
    for p in range(PARTS):
        mine[p] = partial(everything, col, p)
    for p in range(PARTS):
        own_sib(p).wait_recv()
        mine[p] += own_r[p].astype(F32)
    for h in range(2):
        for p in range(PARTS):
            to_cross(h, p).wait_recv()
            out_ref[token_rows(h), p * part:(p + 1) * part] = (
                mine[p, token_rows(h)] + cross_r[h, p].astype(F32)
            ).astype(BF)
    for p in range(PARTS):
        own_sib(p).wait_send()
        for h in range(2):
            to_sib(h, p).wait_send()
            to_cross(h, p).wait_send()

    landed(send_f, fwd_send.at[0])
    for q in range(CHUNKS):
        landed(send_p.at[q], fwd_send.at[1 + q])
    landed(ret_s.at[0], ret_send.at[0])
    landed(ret_s.at[1], ret_send.at[1])


def body(queries, keys, values, filters, skip_weight, out_weight):
    n = lax.axis_size("seq")
    tok, width = keys.shape
    cols = width
    half = tok // 2
    chans = width // n
    tables = [jnp.asarray(t) for t in make_tables(n, tok)]
    operands = (
        filters, keys, values, *tables, queries, skip_weight.reshape(1, width), out_weight,
    )
    dma = pltpu.SemaphoreType.DMA
    scratch = [pltpu.VMEM(x.shape, x.dtype) for x in operands] + [
        pltpu.VMEM((n, 2, chans, half), BF),
        pltpu.VMEM((CHUNKS, n, 2 * chans // CHUNKS, half), BF),
        pltpu.VMEM((n, 2, chans, half), BF),
        pltpu.VMEM((CHUNKS, n, 2 * chans // CHUNKS, half), BF),
        pltpu.VMEM((2, n, chans, half), BF),
        pltpu.VMEM((2, n, chans, half), BF),
        pltpu.VMEM((2, n * chans, half), F32),
        pltpu.VMEM((2, n * chans, half), F32),
        pltpu.VMEM((n * chans, 2 * tok), BF),
        pltpu.VMEM((n * chans, 2 * tok), BF),
        pltpu.VMEM((2, n * chans, tok), F32),
        pltpu.VMEM((n * chans, 2 * tok), F32),
        pltpu.VMEM((tok, width), BF),
        pltpu.VMEM((PARTS, tok, cols // PARTS), F32),
        pltpu.VMEM((2, PARTS, half, cols // PARTS), BF),
        pltpu.VMEM((2, PARTS, half, cols // PARTS), BF),
        pltpu.VMEM((PARTS, tok, cols // PARTS), BF),
        pltpu.VMEM((PARTS, tok, cols // PARTS), BF),
        pltpu.VMEM((2, PARTS, half, cols // PARTS), BF),
        pltpu.VMEM((2, PARTS, half, cols // PARTS), BF),
        dma((16,)),
        dma((1 + CHUNKS,)),
        dma((1 + CHUNKS,)),
        dma((2,)),
        dma((2,)),
        dma((5 * PARTS,)),
        dma((5 * PARTS,)),
    ]
    flops = 2 * chans * n * 3 * (2 * tok) * tok * 3 + 2 * tok * width * 4 * cols
    return pl.pallas_call(
        kernel,
        out_shape=jax.ShapeDtypeStruct((tok, cols), BF),
        in_specs=[pl.BlockSpec(memory_space=pl.ANY)] * len(operands),
        out_specs=pl.BlockSpec(memory_space=pltpu.VMEM),
        scratch_shapes=scratch,
        compiler_params=pltpu.CompilerParams(
            collective_id=0, has_side_effects=True, vmem_limit_bytes=62 * 1024 * 1024
        ),
        cost_estimate=pl.CostEstimate(
            flops=flops, bytes_accessed=16 * 1024 * 1024, transcendentals=0
        ),
        name="hyena",
    )(*operands)


def solution(mesh):
    in_specs = (
        P("seq", "fsdp"),
        P("seq", "fsdp"),
        P("seq", "fsdp"),
        P("seq", "fsdp"),
        P("fsdp"),
        P("fsdp", None),
    )
    out_specs = P("seq", "fsdp")
    return jax.shard_map(body, mesh=mesh, in_specs=in_specs, out_specs=out_specs, check_vma=False)
```
